128 devices in a mesh: blk: 64 (over x, y_hi, z, core), rhs: 2 (over y_lo).
Axes of the slice: x: 4, y: 4 (y_hi: 2, y_lo: 2; y = y_hi * 2 + y_lo), z: 4, core: 2. Of those that a mesh axis runs over, the one named last changes fastest.
Arguments:
- rhs_vectors: float32 [64, 1048576], P('rhs', 'blk'), may hold values from -6 to 6
- leaf_basis: bfloat16 [8192, 32, 128], P('blk'), may hold values from -0.5 to 0.5
- leaf_expand: bfloat16 [8192, 32, 128], P(('blk', 'rhs')), may hold values from -1 to 1
- outer_levels: bfloat16 [7, 8192, 2048], P(None, 'blk'), may hold values from -0.75 to 0.75
- inner_levels: bfloat16 [6, 8192, 2048], P(None, ('blk', 'rhs')), may hold values from -0.75 to 0.75
- near_blocks: bfloat16 [8192, 3, 128, 128], P('blk'), may hold values from -0.3125 to 0.3125
- near_list: int32 [8192, 3], P('blk'), may hold values from 0 to 8191, as said below
Outputs:
- applied: float32 [64, 1048576], P('rhs', 'blk')
The draws below stay inside these ranges and needn't reach their ends.
Inputs may be any that keep to these rules, and one draw needn't show every extreme that they name: near_list[b, 0] = b, near_list[b, 1] is one or two boxes before b and near_list[b, 2] one or two boxes after b, counted around the closed boundary of 8192 boxes.
All inputs are finite; a program needn't handle non-finite values.
Results may differ from the reference program's by a relative error of at most 0.0029.
Values may be sent and summed in bfloat16 or wider, within the bound.
No kernel may reach another device: no remote copies, remote signals or barrier semaphores. Data moves between devices by JAX's collectives and lax.ppermute only.
A program may use at most 128 MiB of HBM per device.

```python
import jax
import jax.numpy as jnp
from jax import lax

LEAF = 128
K = 32
NB = 3
R = 64
BOX_DEV = 128
BOX_LEVELS = 7
MID_LEVELS = 6
GROUP = 2
NBOX = 8192
POINTS = 1048576
N_BLK = 64


def draw_near_list(key, part):
    key = jax.random.fold_in(key, 7)
    steps = jax.random.randint(key, (NBOX, 2), 0, 2).astype(jnp.int32)
    boxes = jnp.arange(NBOX, dtype=jnp.int32)
    before = jnp.mod(boxes - 1 - steps[:, 0], NBOX)
    after = jnp.mod(boxes + 1 + steps[:, 1], NBOX)
    return jnp.stack([boxes, before, after], axis=1).astype(jnp.int32)


def block_levels(rng, extent, cuts, low, high):
    gain, own = 1.0, jax.random.fold_in(rng, 6)
    for position, parts in cuts:
        draws = jnp.exp(jax.random.uniform(jax.random.fold_in(own, position), (parts,), jnp.float32, low / len(cuts), high / len(cuts)))
        gain = gain * jnp.repeat(draws, extent[position] // parts).reshape([-1 if axis == position else 1 for axis in range(len(extent))])
    return gain


def bell_draw(rng, shape, scale, limit, split=(), kind=jnp.bfloat16):
    level = block_levels(rng, shape, split, -0.22, 0.18) if split else 1.0
    array = jax.random.normal(rng, shape, jnp.float32) * scale * level
    return jnp.minimum(jnp.maximum(array, -limit), limit).astype(kind)


def setup_inputs(seed: int = 0) -> dict:
    key_of = jax.random.split(jax.random.key(seed), 8)
    rhs_vectors = bell_draw(key_of[0], (R, POINTS), 1.0, 6.0, ((0, 2), (1, 64)), jnp.float32)
    leaf_basis = bell_draw(key_of[1], (NBOX, K, LEAF), LEAF ** -0.5, 0.5, ((0, 64),))
    leaf_expand = bell_draw(key_of[2], (NBOX, K, LEAF), K ** -0.5, 1.0, ((0, 128),))
    outer_levels = bell_draw(key_of[3], (BOX_LEVELS, NBOX, 2 * K * K), (2 * K) ** -0.5, 0.75, ((1, 64),))
    inner_levels = bell_draw(key_of[4], (MID_LEVELS, NBOX, 2 * K * K), (2 * K) ** -0.5, 0.75, ((1, 128),))
    near_blocks = bell_draw(key_of[5], (NBOX, NB, LEAF, LEAF), (NB * LEAF) ** -0.5, 0.3125, ((0, 64),))
    near_list = draw_near_list(jax.random.fold_in(key_of[7], 71), 0)
    return {"rhs_vectors": rhs_vectors, "leaf_basis": leaf_basis, "leaf_expand": leaf_expand, "outer_levels": outer_levels, "inner_levels": inner_levels, "near_blocks": near_blocks, "near_list": near_list}


def refine(state, factors):
    quads, freqs, cols, rank = state.shape
    pairs = quads // 2
    blocks = factors.astype(jnp.float32).reshape(pairs, 2 * freqs, 2, rank, rank)
    kids = state.reshape(pairs, 2, freqs, cols, rank)
    spread = jnp.repeat(kids, 2, axis=2)
    return jnp.einsum('qfckj,qcfrj->qfrk', blocks, spread, precision=lax.Precision.HIGHEST)


def split_refine(state, factors):
    quads, halves, freqs, cols, rank = state.shape
    pairs = quads // 2
    blocks = factors.astype(jnp.float32).reshape(2, pairs, 2 * freqs, 2, rank, rank)
    kids = state.reshape(pairs, 2, 2, freqs, cols, rank)
    spread = jnp.repeat(kids, 2, axis=3)
    return jnp.einsum('hqfckj,qchfrj->qhfrk', blocks, spread, precision=lax.Precision.HIGHEST)


def reference(rhs_vectors, leaf_basis, leaf_expand, outer_levels, inner_levels, near_blocks, near_list):
    xb = rhs_vectors.astype(jnp.bfloat16)
    boxed = xb.reshape(R, NBOX, LEAF)
    coeff = jnp.einsum('bkp,rbp->brk', leaf_basis.astype(jnp.float32), boxed.astype(jnp.float32), precision=lax.Precision.HIGHEST)
    state = coeff.reshape(N_BLK, BOX_DEV, 1, R, K)
    for level in range(BOX_LEVELS):
        state = jax.vmap(refine)(state, outer_levels[level].reshape(N_BLK, BOX_DEV, 2 * K * K))
    middle = state.reshape(N_BLK, N_BLK, 2, GROUP // 2, R, K)
    inner = jnp.transpose(middle, (1, 0, 2, 3, 4, 5))
    for level in range(MID_LEVELS):
        inner = jax.vmap(split_refine)(inner, inner_levels[level].reshape(N_BLK, BOX_DEV, 2 * K * K))
    target = inner.reshape(NBOX, R, K)
    far = jnp.einsum('bkp,brk->rbp', leaf_expand.astype(jnp.float32), target, precision=lax.Precision.HIGHEST)

    def near_block(pair):
        blocks, lists = pair
        pieces = jnp.take(boxed, lists, axis=1).astype(jnp.float32)
        return jnp.einsum('bjpq,rbjq->rbp', blocks.astype(jnp.float32), pieces, precision=lax.Precision.HIGHEST)

    near = lax.map(near_block, (near_blocks.reshape(N_BLK, BOX_DEV, NB, LEAF, LEAF), near_list.reshape(N_BLK, BOX_DEV, NB)))
    near = jnp.transpose(near, (1, 0, 2, 3)).reshape(R, NBOX, LEAF)
    return (far + near).reshape(R, POINTS)
```

```python
import jax
import jax.numpy as jnp
from jax import lax
from jax.experimental import pallas as pl
from jax.experimental.pallas import tpu as pltpu
from jax.sharding import PartitionSpec as P

RANK = 32
LEAF = 128
COLS = 32
F32 = jnp.float32
BF16 = jnp.bfloat16
NT = (((1,), (1,)), ((), ()))


def lane_block():
    return lax.broadcasted_iota(jnp.int32, (8, 128), 1) // RANK


def spread_factors(factors, rows):
    def run(first):
        block = lane_block()
        even = (block % 2) == 0
        left = block < 2
        for high in range(RANK // 4):
            pair0 = factors[pl.ds(first, 16), pl.ds(high * 128, 128)].astype(F32)
            pair1 = factors[pl.ds(first, 16), pl.ds(1024 + high * 128, 128)].astype(F32)
            for part in range(2):
                kid0 = pair0[part * 8 : part * 8 + 8]
                kid1 = pair1[part * 8 : part * 8 + 8]
                outer = jnp.where(even, kid0, pltpu.roll(kid1, 32, 1))
                inner = jnp.where(even, pltpu.roll(kid0, 96, 1), kid1)
                outer_swap = pltpu.roll(outer, 64, 1)
                inner_swap = pltpu.roll(inner, 64, 1)
                lines = (
                    jnp.where(left, outer, outer_swap),
                    jnp.where(left, inner, inner_swap),
                    jnp.where(left, outer_swap, outer),
                    jnp.where(left, inner_swap, inner),
                )
                for low in range(4):
                    start = (first + part * 8) * RANK + high * 4 + low
                    rows[pl.ds(start, 8, stride=RANK), :] = lines[low]

    return run


def split(value):
    high = value.astype(BF16)
    return high, (value - high.astype(F32)).astype(BF16)


def group_product(index, freqs, rows, high, low):
    kid0 = (2 * index - (index & (freqs - 1))) * RANK
    kid1 = kid0 + freqs * RANK
    kid0 = pl.multiple_of(kid0, RANK)
    kid1 = pl.multiple_of(kid1, RANK)
    left = rows[pl.ds(index * 2 * RANK, 2 * RANK), :].astype(BF16)
    right = jnp.concatenate(
        [
            high[pl.ds(kid0, RANK), :],
            high[pl.ds(kid1, RANK), :],
            low[pl.ds(kid0, RANK), :],
            low[pl.ds(kid1, RANK), :],
        ],
        axis=0,
    )
    return jnp.dot(left, right, preferred_element_type=F32)


def run_level(groups, freqs, factors, rows, source, target, finish=None):
    spread = spread_factors(factors, rows)
    for first in range(0, 2 * groups, 16):
        spread(first)
        for index in range(first // 2, first // 2 + 8):
            value = group_product(index, freqs, rows, source[0], source[1])
            if finish is None:
                top, rest = split(value)
                target[0][pl.ds(index * 2 * RANK, 2 * RANK), :] = top
                target[1][pl.ds(index * 2 * RANK, 2 * RANK), :] = rest
            else:
                finish(index, value)


LEAF_STEPS = 4


def outer_kernel(rhs, basis, factors, boxes_out, out, rows, high0, low0, high1, low1):
    step = pl.program_id(0)
    levels = pl.num_programs(0) - LEAF_STEPS
    level = step - LEAF_STEPS

    @pl.when(step < LEAF_STEPS)
    def _():
        count = basis.shape[0]
        base = step * count * RANK
        for box in range(count):
            piece = rhs[:, pl.ds(box * LEAF, LEAF)].astype(BF16)
            boxes_out[box] = piece
            value = lax.dot_general(basis[box], piece, NT, preferred_element_type=F32)
            top, rest = split(value)
            at = pl.multiple_of(base + box * RANK, RANK)
            high0[pl.ds(at, RANK), :] = top
            low0[pl.ds(at, RANK), :] = rest

    groups = high0.shape[0] // (2 * RANK)
    freqs = lax.shift_left(jnp.int32(1), jnp.maximum(level, 0))
    inside = (level >= 0) & (level < levels - 1)
    factor = factors.at[0]

    @pl.when(inside & (level % 2 == 0))
    def _():
        run_level(groups, freqs, factor, rows, (high0, low0), (high1, low1))

    @pl.when(inside & (level % 2 == 1))
    def _():
        run_level(groups, freqs, factor, rows, (high1, low1), (high0, low0))

    @pl.when(level == levels - 1)
    def _():
        def pack(index, value):
            parts = []
            for freq in range(2):
                lines = [
                    value[freq * RANK + 8 * part : freq * RANK + 8 * part + 8] for part in range(4)
                ]
                parts.append(jnp.concatenate(lines, axis=1))
            out[pl.ds(index * 16, 16), :] = jnp.concatenate(parts, axis=0).astype(BF16)

        run_level(groups, freqs, factor, rows, (high0, low0), None, pack)


def outer(rhs, basis, factors):
    boxes = basis.shape[0]
    levels = factors.shape[0]
    per = boxes // LEAF_STEPS
    last = LEAF_STEPS - 1
    state = pltpu.VMEM((boxes * RANK, COLS), BF16)
    return pl.pallas_call(
        outer_kernel,
        grid=(LEAF_STEPS + levels,),
        in_specs=[
            pl.BlockSpec((COLS, per * LEAF), lambda i: (0, jnp.minimum(i, last))),
            pl.BlockSpec((per, RANK, LEAF), lambda i: (jnp.minimum(i, last), 0, 0)),
            pl.BlockSpec(
                (1, boxes, 2 * RANK * RANK), lambda i: (jnp.maximum(i - LEAF_STEPS, 0), 0, 0)
            ),
        ],
        out_specs=[
            pl.BlockSpec((per, COLS, LEAF), lambda i: (jnp.minimum(i, last), 0, 0)),
            pl.BlockSpec((boxes * 8, 128), lambda i: (0, 0)),
        ],
        out_shape=[
            jax.ShapeDtypeStruct((boxes, COLS, LEAF), BF16),
            jax.ShapeDtypeStruct((boxes * 8, 128), BF16),
        ],
        scratch_shapes=[pltpu.VMEM((boxes * RANK, 128), F32), state, state, state, state],
        compiler_params=pltpu.CompilerParams(vmem_limit_bytes=56 * 2**20),
        cost_estimate=pl.CostEstimate(
            flops=4 * 10**8, bytes_accessed=8 * 10**6, transcendentals=0
        ),
        name="outer_levels",
    )(rhs, basis, factors)


def near_kernel(index, blocks, boxes, low, high, out, wide):
    step = pl.program_id(0)
    count = boxes.shape[0]
    per = blocks.shape[0]

    @pl.when(step == 0)
    def _():
        wide[pl.ds(2, count)] = boxes[...]
        for side in range(2):
            wide[side] = low[:, side * LEAF : (side + 1) * LEAF]
            wide[count + 2 + side] = high[:, side * LEAF : (side + 1) * LEAF]

    for box in range(per):
        total = None
        for side in range(3):
            piece = wide[index[(step * per + box) * 3 + side]]
            term = lax.dot_general(piece, blocks[box, side], NT, preferred_element_type=F32)
            total = term if total is None else total + term
        out[:, box * LEAF : (box + 1) * LEAF] = total


def near_field(index, blocks, boxes, low, high):
    count = blocks.shape[0]
    per = 8
    return pl.pallas_call(
        near_kernel,
        grid_spec=pltpu.PrefetchScalarGridSpec(
            num_scalar_prefetch=1,
            grid=(count // per,),
            in_specs=[
                pl.BlockSpec((per, 3, LEAF, LEAF), lambda i, s: (i, 0, 0, 0)),
                pl.BlockSpec((count, COLS, LEAF), lambda i, s: (0, 0, 0)),
                pl.BlockSpec((COLS, 2 * LEAF), lambda i, s: (0, 0)),
                pl.BlockSpec((COLS, 2 * LEAF), lambda i, s: (0, 0)),
            ],
            out_specs=pl.BlockSpec((COLS, per * LEAF), lambda i, s: (0, i)),
            scratch_shapes=[pltpu.VMEM((count + 4, COLS, LEAF), BF16)],
        ),
        out_shape=jax.ShapeDtypeStruct((COLS, count * LEAF), F32),
        compiler_params=pltpu.CompilerParams(vmem_limit_bytes=56 * 2**20),
        cost_estimate=pl.CostEstimate(
            flops=5 * 10**8, bytes_accessed=16 * 10**6, transcendentals=0
        ),
        name="near_field",
    )(index, blocks, boxes, low, high)


def inner_kernel(side, arrived, factors, own, sent, rows, high0, low0, high1, low1):
    level = pl.program_id(0)
    levels = pl.num_programs(0)
    sources = arrived.shape[0] // 16
    groups = sources // 2

    @pl.when(level == 0)
    def _():
        block = lane_block()
        for source in range(sources):
            both = arrived[pl.ds(source * 16, 16), :].astype(F32)
            first, second = both[:8], both[8:]
            parts = []
            for part in range(4):
                left = first if part == 0 else pltpu.roll(first, 128 - 32 * part, 1)
                right = second if part == 1 else pltpu.roll(second, (160 - 32 * part) % 128, 1)
                parts.append(jnp.where(block == 0, left, right)[:, : 2 * COLS])
            high0[pl.ds(source * RANK, RANK), :] = jnp.concatenate(parts, axis=0).astype(BF16)
        low0[...] = jnp.zeros_like(low0)

    freqs = lax.shift_left(jnp.int32(1), level)
    factor = factors.at[0]

    @pl.when((level < levels - 1) & (level % 2 == 0))
    def _():
        run_level(groups, freqs, factor, rows, (high0, low0), (high1, low1))

    @pl.when((level < levels - 1) & (level % 2 == 1))
    def _():
        run_level(groups, freqs, factor, rows, (high1, low1), (high0, low0))

    @pl.when(level == levels - 1)
    def _():
        kept = {}
        mine = side[0] == 0

        def pack(index, value):
            kept[index] = value
            if index % 2 == 0:
                return
            pieces = [
                kept[index - 1][:RANK],
                kept[index - 1][RANK:],
                kept[index][:RANK],
                kept[index][RANK:],
            ]
            first = jnp.concatenate([piece[:, :COLS] for piece in pieces], axis=1)
            second = jnp.concatenate([piece[:, COLS:] for piece in pieces], axis=1)
            own[index // 2] = jnp.where(mine, first, second).astype(BF16)
            sent[index // 2] = jnp.where(mine, second, first).astype(BF16)

        run_level(groups, freqs, factor, rows, (high1, low1), None, pack)


def inner(side, arrived, factors):
    levels, sources, width = factors.shape
    state = pltpu.VMEM((sources * RANK, 2 * COLS), BF16)
    packed = jax.ShapeDtypeStruct((sources // 4, RANK, 128), BF16)
    whole = pl.BlockSpec((sources // 4, RANK, 128), lambda i, s: (0, 0, 0))
    return pl.pallas_call(
        inner_kernel,
        grid_spec=pltpu.PrefetchScalarGridSpec(
            num_scalar_prefetch=1,
            grid=(levels,),
            in_specs=[
                pl.BlockSpec(arrived.shape, lambda i, s: (0, 0)),
                pl.BlockSpec((1, sources, width), lambda i, s: (i, 0, 0)),
            ],
            out_specs=[whole, whole],
            scratch_shapes=[pltpu.VMEM((sources * RANK, 128), F32), state, state, state, state],
        ),
        out_shape=[packed, packed],
        compiler_params=pltpu.CompilerParams(vmem_limit_bytes=56 * 2**20),
        cost_estimate=pl.CostEstimate(
            flops=2 * 10**8, bytes_accessed=2 * 10**6, transcendentals=0
        ),
        name="inner_levels",
    )(side, arrived, factors)


def expand_kernel(side, coeffs, expand, near, out):
    for quad in range(coeffs.shape[0]):
        turned = coeffs[quad].astype(F32).T.astype(BF16)
        for part in range(4):
            box = quad * 4 + part
            value = jnp.dot(
                turned[part * COLS : (part + 1) * COLS],
                expand[box],
                preferred_element_type=F32,
            )
            at = pl.ds(box * LEAF, LEAF)
            out[:, at] = near[:, at] + value


def expand_into(side, coeffs, expand, near):
    boxes = expand.shape[0]
    steps = 4
    per = boxes // steps
    return pl.pallas_call(
        expand_kernel,
        grid_spec=pltpu.PrefetchScalarGridSpec(
            num_scalar_prefetch=1,
            grid=(steps,),
            in_specs=[
                pl.BlockSpec((per // 4, RANK, 128), lambda i, s: (i, 0, 0)),
                pl.BlockSpec((per, RANK, LEAF), lambda i, s: (i, 0, 0)),
                pl.BlockSpec((COLS, per * LEAF), lambda i, s: (0, s[0] * steps + i)),
            ],
            out_specs=pl.BlockSpec((COLS, per * LEAF), lambda i, s: (0, s[0] * steps + i)),
        ),
        out_shape=jax.ShapeDtypeStruct(near.shape, F32),
        input_output_aliases={3: 0},
        compiler_params=pltpu.CompilerParams(vmem_limit_bytes=56 * 2**20),
        cost_estimate=pl.CostEstimate(
            flops=2 * 10**7, bytes_accessed=3 * 10**6, transcendentals=0
        ),
        name="expand_boxes",
    )(side, coeffs, expand, near)


def shards(
    rhs_vectors, leaf_basis, leaf_expand, outer_levels, inner_levels, near_blocks, near_list
):
    box_count = leaf_basis.shape[0]
    blocks = lax.axis_size("blk")
    swap = [(0, 1), (1, 0)]
    side = lax.axis_index("rhs").astype(jnp.int32).reshape(1)

    other_expand = lax.ppermute(leaf_expand, "rhs", swap)
    width = 2 * LEAF
    forward = [(i, (i + 1) % blocks) for i in range(blocks)]
    backward = [(i, (i - 1) % blocks) for i in range(blocks)]
    low = lax.ppermute(rhs_vectors[:, -width:].astype(BF16), "blk", forward)
    high = lax.ppermute(rhs_vectors[:, :width].astype(BF16), "blk", backward)

    total_boxes = box_count * blocks
    first_box = lax.axis_index("blk") * box_count
    local = jnp.arange(box_count, dtype=jnp.int32)
    offsets = jnp.mod(near_list - (first_box + local)[:, None] + total_boxes // 2, total_boxes)
    index = (local[:, None] + 2 + offsets - total_boxes // 2).reshape(-1)

    boxes, outgoing = outer(rhs_vectors, leaf_basis, outer_levels)
    outgoing, low, high, other_expand = lax.optimization_barrier(
        (outgoing, low, high, other_expand)
    )
    arrived = lax.all_to_all(outgoing, ("blk", "rhs"), split_axis=0, concat_axis=0, tiled=True)
    near = near_field(index, near_blocks, boxes, low, high)
    arrived, near = lax.optimization_barrier((arrived, near))
    own, sent = inner(side, arrived, inner_levels)
    other = lax.ppermute(sent, "rhs", swap)
    result = expand_into(side, own, leaf_expand, near)
    return expand_into(1 - side, other, other_expand, result)


def solution(mesh):
    in_specs = (
        P("rhs", "blk"),
        P("blk", None, None),
        P(("blk", "rhs"), None, None),
        P(None, "blk", None),
        P(None, ("blk", "rhs"), None),
        P("blk", None, None, None),
        P("blk", None),
    )
    out_specs = P("rhs", "blk")
    return jax.shard_map(shards, mesh=mesh, in_specs=in_specs, out_specs=out_specs, check_vma=False)
```

```python
import jax
import jax.numpy as jnp
from jax import lax
from jax.experimental import pallas as pl
from jax.experimental.pallas import tpu as pltpu
from jax.sharding import PartitionSpec as P

RANK = 32
LEAF = 128
COLS = 32
F32 = jnp.float32
BF16 = jnp.bfloat16
NT = (((1,), (1,)), ((), ()))


NATURAL = (((0, 0), (1, 32), (2, 32), (3, 64)), ((4, 64), (5, 96), (6, 96), (7, 0)))
PAIRED = (((0, 0), (1, 32), (4, 0), (5, 32)), ((2, 96), (3, 0), (6, 96), (7, 0)))


def lane_block():
    return lax.broadcasted_iota(jnp.int32, (8, 128), 1) // RANK


def pick(choices):
    block = lane_block()
    low = jnp.where(block == 0, choices[0], choices[1])
    high = jnp.where(block == 2, choices[2], choices[3])
    return jnp.where(block < 2, low, high)


def factor_rows(factors, first):
    block = lax.broadcasted_iota(jnp.int32, (16, 128), 1) // RANK
    even = (block % 2) == 0
    left = block < 2
    rows = ([], [])
    for high in range(RANK // 4):
        kid0 = factors[pl.ds(first, 16), pl.ds(high * 128, 128)]
        kid1 = factors[pl.ds(first, 16), pl.ds(1024 + high * 128, 128)]
        outer = jnp.where(even, kid0, pltpu.roll(kid1, 32, 1))
        inner = jnp.where(even, pltpu.roll(kid0, 96, 1), kid1)
        outer_swap = pltpu.roll(outer, 64, 1)
        inner_swap = pltpu.roll(inner, 64, 1)
        for line in (
            jnp.where(left, outer, outer_swap),
            jnp.where(left, inner, inner_swap),
            jnp.where(left, outer_swap, outer),
            jnp.where(left, inner_swap, inner),
        ):
            wide = line.astype(F32)
            rows[0].append(wide[:8])
            rows[1].append(wide[8:])
    return [jnp.concatenate(part, axis=0).astype(BF16) for part in rows]


def split(value):
    high = value.astype(BF16)
    return high, (value - high.astype(F32)).astype(BF16)


def gathered(stage, layout):
    parts = []
    block = lane_block()
    shifts = sorted({shift for _, shift in layout})
    for part in range(4):
        total = None
        for shift in shifts:
            merged = None
            for lane, (freq, amount) in enumerate(layout):
                if amount != shift:
                    continue
                value = stage[pl.ds(part * 64 + freq, 8, stride=8), :]
                source = (lane - shift // 32) % 4
                merged = value if merged is None else jnp.where(block == source, value, merged)
            if shift:
                merged = pltpu.roll(merged, shift, 1)
            if total is None:
                total = merged
            else:
                mask = None
                for lane, (_, amount) in enumerate(layout):
                    if amount == shift:
                        here = block == lane
                        mask = here if mask is None else mask | here
                total = jnp.where(mask, merged, total)
        parts.append(total)
    return jnp.concatenate(parts, axis=0)


def put_state(state, at, value):
    high, low = split(value)
    state[0][at] = high
    state[1][at] = low


def run_level(step, layouts, factors, source, target, stage):
    sets = source[0].shape[0]
    blocks = source[0].shape[1] // 2
    for first in range(0, 8 * blocks, 16):
        both = factor_rows(factors, first)
        for part in range(2):
            m = first // 8 + part
            near = 2 * m - (m & (step - 1))
            far = near + step
            for which in range(sets):
                right = jnp.concatenate(
                    [
                        source[0][which, near],
                        source[0][which, far],
                        source[1][which, near],
                        source[1][which, far],
                    ],
                    axis=0,
                )
                slot = stage.at[m * sets + which]
                slot[...] = jnp.dot(both[part], right, preferred_element_type=F32)
                for half, layout in enumerate(layouts):
                    put_state(target, (which, 2 * m + half), gathered(slot, layout))


def level_step(level):
    return jnp.maximum(lax.shift_left(jnp.int32(1), jnp.maximum(level - 2, 0)), 1)


LEAF_STEPS = 4


def outer_kernel(
    rhs_hbm, basis_hbm, factors_hbm, boxes_out, out, rhs, basis, factors, stage, high0, low0, high1, low1, sems
):
    levels = factors.shape[0]
    count = basis.shape[0]
    per = count // LEAF_STEPS

    def leaf_copies(step):
        columns = pl.ds(pl.multiple_of(step * per * LEAF, LEAF), per * LEAF)
        boxes = pl.ds(step * per, per)
        return (
            pltpu.make_async_copy(rhs_hbm.at[:, columns], rhs.at[:, columns], sems.at[0, step]),
            pltpu.make_async_copy(basis_hbm.at[boxes], basis.at[boxes], sems.at[1, step]),
        )

    def level_copy(level):
        return pltpu.make_async_copy(factors_hbm.at[level], factors.at[level], sems.at[2, level])

    for step in range(LEAF_STEPS):
        for copy in leaf_copies(step):
            copy.start()
    for level in range(levels):
        level_copy(level).start()

    def leaf(step, carry):
        for copy in leaf_copies(step):
            copy.wait()
        for group in range(per // 8):
            first = step * per + group * 8
            at = pl.ds(pl.multiple_of(first * LEAF, LEAF), 8 * LEAF)
            columns = rhs[:, at].astype(BF16)
            pieces = [columns[:, box * LEAF : (box + 1) * LEAF] for box in range(8)]
            for box in range(8):
                boxes_out[first + box] = pieces[box]
            for kid in range(2):
                left = jnp.concatenate([basis[first + kid + 2 * i] for i in range(4)], axis=0)
                right = jnp.concatenate([pieces[kid + 2 * i] for i in range(4)], axis=0)
                value = lax.dot_general(left, right, NT, preferred_element_type=F32)
                parts = []
                for part in range(4):
                    at = [i * RANK + part * 8 for i in range(4)]
                    parts.append(pick([value[i : i + 8] for i in at]))
                at = step * (per // 4) + 2 * group + kid
                put_state((high0, low0), (0, at), jnp.concatenate(parts, axis=0))
        return carry

    lax.fori_loop(0, LEAF_STEPS, leaf, 0)

    even, odd = (high0, low0), (high1, low1)
    level_copy(0).wait()
    run_level(1, PAIRED, factors.at[0], even, odd, stage)

    def two_levels(pair, carry):
        level = 2 * pair + 1
        level_copy(level).wait()
        run_level(level_step(level), NATURAL, factors.at[level], odd, even, stage)
        level_copy(level + 1).wait()
        run_level(level_step(level + 1), NATURAL, factors.at[level + 1], even, odd, stage)
        return carry

    lax.fori_loop(0, (levels - 1) // 2, two_levels, 0)

    for block in range(count // 4):
        value = high1[0, block].astype(F32)
        for pair in range(2):
            parts = []
            for freq in (2 * pair, 2 * pair + 1):
                lines = []
                for part in range(4):
                    shift = (part - freq) * 32 % 128
                    line = value[part * 8 : part * 8 + 8]
                    lines.append(pltpu.roll(line, shift, 1) if shift else line)
                parts.append(pick(lines))
            at = pl.ds((2 * block + pair) * 16, 16)
            out[at, :] = jnp.concatenate(parts, axis=0).astype(BF16)


def outer(rhs, basis, factors):
    boxes = basis.shape[0]
    levels = factors.shape[0]
    state = pltpu.VMEM((1, boxes // 4, RANK, 128), BF16)
    whole = pl.BlockSpec(memory_space=pl.ANY)
    return pl.pallas_call(
        outer_kernel,
        in_specs=[whole, whole, whole],
        out_specs=[pl.BlockSpec(memory_space=pltpu.VMEM), pl.BlockSpec(memory_space=pltpu.VMEM)],
        out_shape=[
            jax.ShapeDtypeStruct((boxes, COLS, LEAF), BF16),
            jax.ShapeDtypeStruct((boxes * 8, 128), BF16),
        ],
        scratch_shapes=[
            pltpu.VMEM(rhs.shape, F32),
            pltpu.VMEM(basis.shape, BF16),
            pltpu.VMEM(factors.shape, BF16),
            pltpu.VMEM((boxes // 8, 256, 128), F32),
            state,
            state,
            state,
            state,
            pltpu.SemaphoreType.DMA((3, max(LEAF_STEPS, levels))),
        ],
        compiler_params=pltpu.CompilerParams(vmem_limit_bytes=56 * 2**20),
        cost_estimate=pl.CostEstimate(
            flops=4 * 10**8, bytes_accessed=8 * 10**6, transcendentals=0
        ),
        name="outer_levels",
    )(rhs, basis, factors)


def near_kernel(index, blocks, boxes, low, high, out, wide):
    step = pl.program_id(0)
    count = boxes.shape[0]
    per = blocks.shape[0]

    @pl.when(step == 0)
    def _():
        wide[pl.ds(2, count)] = boxes[...]
        for side in range(2):
            wide[side] = low[:, side * LEAF : (side + 1) * LEAF].astype(BF16)
            wide[count + 2 + side] = high[:, side * LEAF : (side + 1) * LEAF].astype(BF16)

    for box in range(per):
        pieces = [wide[index[(step * per + box) * 3 + side]] for side in range(3)]
        left = jnp.concatenate(pieces, axis=1)
        right = jnp.concatenate([blocks[box, side] for side in range(3)], axis=1)
        out[:, box * LEAF : (box + 1) * LEAF] = lax.dot_general(
            left, right, NT, preferred_element_type=F32
        )


def near_field(index, blocks, boxes, low, high):
    count = blocks.shape[0]
    per = 8
    return pl.pallas_call(
        near_kernel,
        grid_spec=pltpu.PrefetchScalarGridSpec(
            num_scalar_prefetch=1,
            grid=(count // per,),
            in_specs=[
                pl.BlockSpec((per, 3, LEAF, LEAF), lambda i, s: (i, 0, 0, 0)),
                pl.BlockSpec((count, COLS, LEAF), lambda i, s: (0, 0, 0)),
                pl.BlockSpec((COLS, 2 * LEAF), lambda i, s: (0, 0)),
                pl.BlockSpec((COLS, 2 * LEAF), lambda i, s: (0, 0)),
            ],
            out_specs=pl.BlockSpec((COLS, per * LEAF), lambda i, s: (0, i)),
            scratch_shapes=[pltpu.VMEM((count + 4, COLS, LEAF), BF16)],
        ),
        out_shape=jax.ShapeDtypeStruct((COLS, count * LEAF), F32),
        compiler_params=pltpu.CompilerParams(vmem_limit_bytes=56 * 2**20),
        cost_estimate=pl.CostEstimate(
            flops=5 * 10**8, bytes_accessed=16 * 10**6, transcendentals=0
        ),
        name="near_field",
    )(index, blocks, boxes, low, high)


def inner_kernel(side, arrived, factors_hbm, out, factors, stage, high0, low0, high1, low1, sems):
    levels = factors.shape[0]
    sources = arrived.shape[0] // 16

    def level_copy(level):
        return pltpu.make_async_copy(factors_hbm.at[level], factors.at[level], sems.at[level])

    for level in range(levels):
        level_copy(level).start()

    low0[...] = jnp.zeros_like(low0)
    for first in range(0, sources, 8):
        both = [arrived[pl.ds((first + i) * 16, 16), :].astype(F32) for i in range(8)]
        for which in range(2):
            sent = [value[which * 8 : which * 8 + 8] for value in both]
            for kid in range(2):
                parts = []
                for part in range(4):
                    lines = []
                    for i in range(4):
                        shift = (i - part) * 32 % 128
                        value = sent[kid + 2 * i]
                        lines.append(pltpu.roll(value, shift, 1) if shift else value)
                    parts.append(pick(lines))
                high0[which, first // 4 + kid] = jnp.concatenate(parts, axis=0).astype(BF16)

    even, odd = (high0, low0), (high1, low1)
    level_copy(0).wait()
    run_level(1, PAIRED, factors.at[0], even, odd, stage)

    def two_levels(pair, carry):
        level = 2 * pair + 1
        level_copy(level).wait()
        run_level(level_step(level), NATURAL, factors.at[level], odd, even, stage)
        level_copy(level + 1).wait()
        run_level(level_step(level + 1), NATURAL, factors.at[level + 1], even, odd, stage)
        return carry

    lax.fori_loop(0, (levels - 2) // 2, two_levels, 0)
    level_copy(levels - 1).wait()
    last = factors.at[levels - 1]
    run_level(level_step(levels - 1), NATURAL, last, odd, even, stage)
    for which in range(2):
        out[which ^ side[0]] = high0[which]


def inner(side, arrived, factors):
    levels, sources, _ = factors.shape
    state = pltpu.VMEM((2, sources // 4, RANK, 128), BF16)
    return pl.pallas_call(
        inner_kernel,
        in_specs=[
            pl.BlockSpec(memory_space=pltpu.SMEM),
            pl.BlockSpec(memory_space=pltpu.VMEM),
            pl.BlockSpec(memory_space=pl.ANY),
        ],
        out_specs=pl.BlockSpec(memory_space=pltpu.VMEM),
        out_shape=jax.ShapeDtypeStruct((2, sources // 4, RANK, 128), BF16),
        scratch_shapes=[
            pltpu.VMEM(factors.shape, BF16),
            pltpu.VMEM((sources // 4, 256, 128), F32),
            state,
            state,
            state,
            state,
            pltpu.SemaphoreType.DMA((levels,)),
        ],
        compiler_params=pltpu.CompilerParams(vmem_limit_bytes=56 * 2**20),
        cost_estimate=pl.CostEstimate(
            flops=2 * 10**8, bytes_accessed=2 * 10**6, transcendentals=0
        ),
        name="inner_levels",
    )(side, arrived, factors)


def expand_kernel(side, coeffs, expand, near, out):
    for quad in range(coeffs.shape[0]):
        turned = coeffs[quad].astype(F32).T.astype(BF16)
        for part in range(4):
            box = quad * 4 + part
            value = jnp.dot(
                turned[part * COLS : (part + 1) * COLS],
                expand[box],
                preferred_element_type=F32,
            )
            at = pl.ds(box * LEAF, LEAF)
            out[:, at] = near[:, at] + value


def expand_into(side, coeffs, expand, near):
    boxes = expand.shape[0]
    steps = 4
    per = boxes // steps
    return pl.pallas_call(
        expand_kernel,
        grid_spec=pltpu.PrefetchScalarGridSpec(
            num_scalar_prefetch=1,
            grid=(steps,),
            in_specs=[
                pl.BlockSpec((per // 4, RANK, 128), lambda i, s: (i, 0, 0)),
                pl.BlockSpec((per, RANK, LEAF), lambda i, s: (i, 0, 0)),
                pl.BlockSpec((COLS, per * LEAF), lambda i, s: (0, s[0] * steps + i)),
            ],
            out_specs=pl.BlockSpec((COLS, per * LEAF), lambda i, s: (0, s[0] * steps + i)),
        ),
        out_shape=jax.ShapeDtypeStruct(near.shape, F32),
        input_output_aliases={3: 0},
        compiler_params=pltpu.CompilerParams(vmem_limit_bytes=8 * 2**20),
        cost_estimate=pl.CostEstimate(
            flops=2 * 10**7, bytes_accessed=3 * 10**6, transcendentals=0
        ),
        name="expand_boxes",
    )(side, coeffs, expand, near)


def shards(
    rhs_vectors, leaf_basis, leaf_expand, outer_levels, inner_levels, near_blocks, near_list
):
    box_count = leaf_basis.shape[0]
    blocks = lax.axis_size("blk")
    swap = [(0, 1), (1, 0)]
    side = lax.axis_index("rhs").astype(jnp.int32).reshape(1)

    width = 2 * LEAF
    forward = [(i, (i + 1) % blocks) for i in range(blocks)]
    backward = [(i, (i - 1) % blocks) for i in range(blocks)]
    low = lax.ppermute(rhs_vectors[:, -width:], "blk", forward)
    high = lax.ppermute(rhs_vectors[:, :width], "blk", backward)

    total_boxes = box_count * blocks
    first_box = lax.axis_index("blk") * box_count
    local = jnp.arange(box_count, dtype=jnp.int32)
    offsets = jnp.mod(near_list - (first_box + local)[:, None] + total_boxes // 2, total_boxes)
    index = (local[:, None] + 2 + offsets - total_boxes // 2).reshape(-1)

    boxes, outgoing = outer(rhs_vectors, leaf_basis, outer_levels)
    outgoing, low, high, own_expand = lax.optimization_barrier((outgoing, low, high, leaf_expand))
    other_expand = lax.ppermute(own_expand, "rhs", swap)
    arrived = lax.all_to_all(outgoing, ("blk", "rhs"), split_axis=0, concat_axis=0, tiled=True)
    near = near_field(index, near_blocks, boxes, low, high)
    arrived, near = lax.optimization_barrier((arrived, near))
    coeffs = inner(side, arrived, inner_levels)
    other = lax.ppermute(coeffs[1], "rhs", swap)
    result = expand_into(side, coeffs[0], leaf_expand, near)
    return expand_into(1 - side, other, other_expand, result)


def solution(mesh):
    in_specs = (
        P("rhs", "blk"),
        P("blk", None, None),
        P(("blk", "rhs"), None, None),
        P(None, "blk", None),
        P(None, ("blk", "rhs"), None),
        P("blk", None, None, None),
        P("blk", None),
    )
    out_specs = P("rhs", "blk")
    return jax.shard_map(shards, mesh=mesh, in_specs=in_specs, out_specs=out_specs, check_vma=False)
```

```python
import jax
import jax.numpy as jnp
from jax import lax
from jax.experimental import pallas as pl
from jax.experimental.pallas import tpu as pltpu
from jax.sharding import PartitionSpec as P

RANK = 32
LEAF = 128
COLS = 32
F32 = jnp.float32
BF16 = jnp.bfloat16
NT = (((1,), (1,)), ((), ()))


NATURAL = (((0, 0), (1, 32), (2, 32), (3, 64)), ((4, 64), (5, 96), (6, 96), (7, 0)))
PAIRED = (((0, 0), (1, 32), (4, 0), (5, 32)), ((2, 96), (3, 0), (6, 96), (7, 0)))


def lane_block():
    return lax.broadcasted_iota(jnp.int32, (8, 128), 1) // RANK


def pick(choices):
    block = lane_block()
    low = jnp.where(block == 0, choices[0], choices[1])
    high = jnp.where(block == 2, choices[2], choices[3])
    return jnp.where(block < 2, low, high)


def factor_rows(factors, first):
    block = lax.broadcasted_iota(jnp.int32, (16, 128), 1) // RANK
    even = (block % 2) == 0
    left = block < 2
    rows = ([], [])
    for high in range(RANK // 4):
        kid0 = factors[pl.ds(first, 16), pl.ds(high * 128, 128)]
        kid1 = factors[pl.ds(first, 16), pl.ds(1024 + high * 128, 128)]
        outer = jnp.where(even, kid0, pltpu.roll(kid1, 32, 1))
        inner = jnp.where(even, pltpu.roll(kid0, 96, 1), kid1)
        outer_swap = pltpu.roll(outer, 64, 1)
        inner_swap = pltpu.roll(inner, 64, 1)
        for line in (
            jnp.where(left, outer, outer_swap),
            jnp.where(left, inner, inner_swap),
            jnp.where(left, outer_swap, outer),
            jnp.where(left, inner_swap, inner),
        ):
            wide = line.astype(F32)
            rows[0].append(wide[:8])
            rows[1].append(wide[8:])
    return [jnp.concatenate(part, axis=0).astype(BF16) for part in rows]


def split(value):
    high = value.astype(BF16)
    return high, (value - high.astype(F32)).astype(BF16)


def gathered(stage, layout):
    parts = []
    block = lane_block()
    shifts = sorted({shift for _, shift in layout})
    for part in range(4):
        total = None
        for shift in shifts:
            merged = None
            for lane, (freq, amount) in enumerate(layout):
                if amount != shift:
                    continue
                value = stage[pl.ds(part * 64 + freq, 8, stride=8), :]
                source = (lane - shift // 32) % 4
                merged = value if merged is None else jnp.where(block == source, value, merged)
            if shift:
                merged = pltpu.roll(merged, shift, 1)
            if total is None:
                total = merged
            else:
                mask = None
                for lane, (_, amount) in enumerate(layout):
                    if amount == shift:
                        here = block == lane
                        mask = here if mask is None else mask | here
                total = jnp.where(mask, merged, total)
        parts.append(total)
    return jnp.concatenate(parts, axis=0)


def put_state(state, at, value):
    high, low = split(value)
    state[0][at] = high
    state[1][at] = low


def run_level(step, layouts, factors, source, target, stage):
    sets = source[0].shape[0]
    blocks = source[0].shape[1] // 2
    for first in range(0, 8 * blocks, 16):
        both = factor_rows(factors, first)
        for part in range(2):
            m = first // 8 + part
            near = 2 * m - (m & (step - 1))
            far = near + step
            for which in range(sets):
                right = jnp.concatenate(
                    [
                        source[0][which, near],
                        source[0][which, far],
                        source[1][which, near],
                        source[1][which, far],
                    ],
                    axis=0,
                )
                slot = stage.at[m * sets + which]
                slot[...] = jnp.dot(both[part], right, preferred_element_type=F32)
                for half, layout in enumerate(layouts):
                    put_state(target, (which, 2 * m + half), gathered(slot, layout))


def level_step(level):
    return jnp.maximum(lax.shift_left(jnp.int32(1), jnp.maximum(level - 2, 0)), 1)


LEAF_STEPS = 4


def outer_kernel(
    rhs_hbm, basis_hbm, factors_hbm, boxes_out, out, rhs, basis, factors, stage, high0, low0, high1, low1, sems
):
    levels = factors.shape[0]
    count = basis.shape[0]
    per = count // LEAF_STEPS

    def leaf_copies(step):
        columns = pl.ds(pl.multiple_of(step * per * LEAF, LEAF), per * LEAF)
        boxes = pl.ds(step * per, per)
        return (
            pltpu.make_async_copy(rhs_hbm.at[:, columns], rhs.at[:, columns], sems.at[0, step]),
            pltpu.make_async_copy(basis_hbm.at[boxes], basis.at[boxes], sems.at[1, step]),
        )

    def level_copy(level):
        return pltpu.make_async_copy(factors_hbm.at[level], factors.at[level], sems.at[2, level])

    for step in range(LEAF_STEPS):
        for copy in leaf_copies(step):
            copy.start()
    for level in range(levels):
        level_copy(level).start()

    def leaf(step, carry):
        for copy in leaf_copies(step):
            copy.wait()
        for group in range(per // 8):
            first = step * per + group * 8
            at = pl.ds(pl.multiple_of(first * LEAF, LEAF), 8 * LEAF)
            columns = rhs[:, at].astype(BF16)
            pieces = [columns[:, box * LEAF : (box + 1) * LEAF] for box in range(8)]
            for box in range(8):
                boxes_out[first + box] = pieces[box]
            for kid in range(2):
                left = jnp.concatenate([basis[first + kid + 2 * i] for i in range(4)], axis=0)
                right = jnp.concatenate([pieces[kid + 2 * i] for i in range(4)], axis=0)
                value = lax.dot_general(left, right, NT, preferred_element_type=F32)
                parts = []
                for part in range(4):
                    at = [i * RANK + part * 8 for i in range(4)]
                    parts.append(pick([value[i : i + 8] for i in at]))
                at = step * (per // 4) + 2 * group + kid
                put_state((high0, low0), (0, at), jnp.concatenate(parts, axis=0))
        return carry

    lax.fori_loop(0, LEAF_STEPS, leaf, 0)

    even, odd = (high0, low0), (high1, low1)
    level_copy(0).wait()
    run_level(1, PAIRED, factors.at[0], even, odd, stage)

    def two_levels(pair, carry):
        level = 2 * pair + 1
        level_copy(level).wait()
        run_level(level_step(level), NATURAL, factors.at[level], odd, even, stage)
        level_copy(level + 1).wait()
        run_level(level_step(level + 1), NATURAL, factors.at[level + 1], even, odd, stage)
        return carry

    lax.fori_loop(0, (levels - 1) // 2, two_levels, 0)

    for block in range(count // 4):
        value = high1[0, block].astype(F32)
        for pair in range(2):
            parts = []
            for freq in (2 * pair, 2 * pair + 1):
                lines = []
                for part in range(4):
                    shift = (part - freq) * 32 % 128
                    line = value[part * 8 : part * 8 + 8]
                    lines.append(pltpu.roll(line, shift, 1) if shift else line)
                parts.append(pick(lines))
            at = pl.ds((2 * block + pair) * 16, 16)
            out[at, :] = jnp.concatenate(parts, axis=0).astype(BF16)


def outer(rhs, basis, factors):
    boxes = basis.shape[0]
    levels = factors.shape[0]
    state = pltpu.VMEM((1, boxes // 4, RANK, 128), BF16)
    whole = pl.BlockSpec(memory_space=pl.ANY)
    return pl.pallas_call(
        outer_kernel,
        in_specs=[whole, whole, whole],
        out_specs=[pl.BlockSpec(memory_space=pltpu.VMEM), pl.BlockSpec(memory_space=pltpu.VMEM)],
        out_shape=[
            jax.ShapeDtypeStruct((boxes, COLS, LEAF), BF16),
            jax.ShapeDtypeStruct((boxes * 8, 128), BF16),
        ],
        scratch_shapes=[
            pltpu.VMEM(rhs.shape, F32),
            pltpu.VMEM(basis.shape, BF16),
            pltpu.VMEM(factors.shape, BF16),
            pltpu.VMEM((boxes // 8, 256, 128), F32),
            state,
            state,
            state,
            state,
            pltpu.SemaphoreType.DMA((3, max(LEAF_STEPS, levels))),
        ],
        compiler_params=pltpu.CompilerParams(vmem_limit_bytes=56 * 2**20),
        cost_estimate=pl.CostEstimate(
            flops=4 * 10**8, bytes_accessed=8 * 10**6, transcendentals=0
        ),
        name="outer_levels",
    )(rhs, basis, factors)


NEAR_STEPS = 16


def near_kernel(index, blocks_hbm, boxes, low, high, out_hbm, wide, blocks, total, sems):
    count = boxes.shape[0]
    per = count // NEAR_STEPS

    def load(step):
        at = pl.ds(step * per, per)
        return pltpu.make_async_copy(blocks_hbm.at[at], blocks.at[at], sems.at[0, step])

    def store(step):
        at = pl.ds(pl.multiple_of(step * per * LEAF, LEAF), per * LEAF)
        return pltpu.make_async_copy(total.at[:, at], out_hbm.at[:, at], sems.at[1, step])

    for step in range(NEAR_STEPS):
        load(step).start()
    wide[pl.ds(2, count)] = boxes[...]
    for side in range(2):
        wide[side] = low[:, side * LEAF : (side + 1) * LEAF].astype(BF16)
        wide[count + 2 + side] = high[:, side * LEAF : (side + 1) * LEAF].astype(BF16)

    def body(step, carry):
        load(step).wait()
        for item in range(per):
            box = step * per + item
            left = jnp.concatenate([wide[index[box * 3 + side]] for side in range(3)], axis=1)
            right = jnp.concatenate([blocks[box, side] for side in range(3)], axis=1)
            at = pl.ds(pl.multiple_of(box * LEAF, LEAF), LEAF)
            total[:, at] = lax.dot_general(left, right, NT, preferred_element_type=F32)
        store(step).start()
        return carry

    lax.fori_loop(0, NEAR_STEPS, body, 0)
    for step in range(NEAR_STEPS):
        store(step).wait()


def near_field(index, blocks, boxes, low, high):
    count = blocks.shape[0]
    vmem = pl.BlockSpec(memory_space=pltpu.VMEM)
    anywhere = pl.BlockSpec(memory_space=pl.ANY)
    return pl.pallas_call(
        near_kernel,
        in_specs=[pl.BlockSpec(memory_space=pltpu.SMEM), anywhere, vmem, vmem, vmem],
        out_specs=anywhere,
        out_shape=jax.ShapeDtypeStruct((COLS, count * LEAF), F32),
        scratch_shapes=[
            pltpu.VMEM((count + 4, COLS, LEAF), BF16),
            pltpu.VMEM(blocks.shape, BF16),
            pltpu.VMEM((COLS, count * LEAF), F32),
            pltpu.SemaphoreType.DMA((2, NEAR_STEPS)),
        ],
        compiler_params=pltpu.CompilerParams(vmem_limit_bytes=56 * 2**20),
        cost_estimate=pl.CostEstimate(
            flops=5 * 10**8, bytes_accessed=16 * 10**6, transcendentals=0
        ),
        name="near_field",
    )(index, blocks, boxes, low, high)


def inner_kernel(side, arrived, factors_hbm, own, sent, factors, stage, high0, low0, high1, low1, sems):
    levels = factors.shape[0]
    sources = arrived.shape[0] // 16

    def level_copy(level):
        return pltpu.make_async_copy(factors_hbm.at[level], factors.at[level], sems.at[level])

    for level in range(levels):
        level_copy(level).start()

    low0[...] = jnp.zeros_like(low0)
    for first in range(0, sources, 8):
        both = [arrived[pl.ds((first + i) * 16, 16), :].astype(F32) for i in range(8)]
        for which in range(2):
            message = [value[which * 8 : which * 8 + 8] for value in both]
            for kid in range(2):
                parts = []
                for part in range(4):
                    lines = []
                    for i in range(4):
                        shift = (i - part) * 32 % 128
                        value = message[kid + 2 * i]
                        lines.append(pltpu.roll(value, shift, 1) if shift else value)
                    parts.append(pick(lines))
                high0[which, first // 4 + kid] = jnp.concatenate(parts, axis=0).astype(BF16)

    even, odd = (high0, low0), (high1, low1)
    level_copy(0).wait()
    run_level(1, PAIRED, factors.at[0], even, odd, stage)

    def two_levels(pair, carry):
        level = 2 * pair + 1
        level_copy(level).wait()
        run_level(level_step(level), NATURAL, factors.at[level], odd, even, stage)
        level_copy(level + 1).wait()
        run_level(level_step(level + 1), NATURAL, factors.at[level + 1], even, odd, stage)
        return carry

    lax.fori_loop(0, (levels - 2) // 2, two_levels, 0)
    level_copy(levels - 1).wait()
    last = factors.at[levels - 1]
    run_level(level_step(levels - 1), NATURAL, last, odd, even, stage)
    own[...] = high0[side[0]]
    sent[...] = high0[1 - side[0]]


def inner(side, arrived, factors):
    levels, sources, _ = factors.shape
    state = pltpu.VMEM((2, sources // 4, RANK, 128), BF16)
    return pl.pallas_call(
        inner_kernel,
        in_specs=[
            pl.BlockSpec(memory_space=pltpu.SMEM),
            pl.BlockSpec(memory_space=pltpu.VMEM),
            pl.BlockSpec(memory_space=pl.ANY),
        ],
        out_specs=[pl.BlockSpec(memory_space=pltpu.VMEM)] * 2,
        out_shape=[jax.ShapeDtypeStruct((sources // 4, RANK, 128), BF16)] * 2,
        scratch_shapes=[
            pltpu.VMEM(factors.shape, BF16),
            pltpu.VMEM((sources // 4, 256, 128), F32),
            state,
            state,
            state,
            state,
            pltpu.SemaphoreType.DMA((levels,)),
        ],
        compiler_params=pltpu.CompilerParams(vmem_limit_bytes=16 * 2**20),
        cost_estimate=pl.CostEstimate(
            flops=2 * 10**8, bytes_accessed=2 * 10**6, transcendentals=0
        ),
        name="inner_levels",
    )(side, arrived, factors)


EXPAND_STEPS = 4


def expand_kernel(side, coeffs, expand_hbm, near_hbm, out_hbm, expand, near, sems):
    boxes = expand.shape[0]
    per = boxes // EXPAND_STEPS
    width = per * LEAF

    def block(step):
        return pl.ds(pl.multiple_of(side[0] * (boxes * LEAF) + step * width, LEAF), width)

    def loads(step):
        at = pl.ds(step * per, per)
        here = pl.ds(step * width, width)
        return (
            pltpu.make_async_copy(expand_hbm.at[at], expand.at[at], sems.at[0, step]),
            pltpu.make_async_copy(near_hbm.at[:, block(step)], near.at[:, here], sems.at[1, step]),
        )

    def store(step):
        here = pl.ds(step * width, width)
        return pltpu.make_async_copy(near.at[:, here], out_hbm.at[:, block(step)], sems.at[2, step])

    for step in range(EXPAND_STEPS):
        for copy in loads(step):
            copy.start()
    turned = [coeffs[quad].astype(F32).T.astype(BF16) for quad in range(boxes // 4)]
    for step in range(EXPAND_STEPS):
        for copy in loads(step):
            copy.wait()
        for box in range(step * per, (step + 1) * per):
            part = box % 4
            at = pl.ds(box * LEAF, LEAF)
            near[:, at] += jnp.dot(
                turned[box // 4][part * COLS : (part + 1) * COLS],
                expand[box],
                preferred_element_type=F32,
            )
        store(step).start()
    for step in range(EXPAND_STEPS):
        store(step).wait()


def expand_into(side, coeffs, expand, near):
    boxes = expand.shape[0]
    anywhere = pl.BlockSpec(memory_space=pl.ANY)
    return pl.pallas_call(
        expand_kernel,
        in_specs=[
            pl.BlockSpec(memory_space=pltpu.SMEM),
            pl.BlockSpec(memory_space=pltpu.VMEM),
            anywhere,
            anywhere,
        ],
        out_specs=anywhere,
        out_shape=jax.ShapeDtypeStruct(near.shape, F32),
        scratch_shapes=[
            pltpu.VMEM(expand.shape, BF16),
            pltpu.VMEM((COLS, boxes * LEAF), F32),
            pltpu.SemaphoreType.DMA((3, EXPAND_STEPS)),
        ],
        input_output_aliases={3: 0},
        compiler_params=pltpu.CompilerParams(vmem_limit_bytes=8 * 2**20),
        cost_estimate=pl.CostEstimate(
            flops=2 * 10**7, bytes_accessed=3 * 10**6, transcendentals=0
        ),
        name="expand_boxes",
    )(side, coeffs, expand, near)


def shards(
    rhs_vectors, leaf_basis, leaf_expand, outer_levels, inner_levels, near_blocks, near_list
):
    box_count = leaf_basis.shape[0]
    blocks = lax.axis_size("blk")
    swap = [(0, 1), (1, 0)]
    side = lax.axis_index("rhs").astype(jnp.int32).reshape(1)

    width = 2 * LEAF
    forward = [(i, (i + 1) % blocks) for i in range(blocks)]
    backward = [(i, (i - 1) % blocks) for i in range(blocks)]
    low = lax.ppermute(rhs_vectors[:, -width:], "blk", forward)
    high = lax.ppermute(rhs_vectors[:, :width], "blk", backward)

    boxes, outgoing = outer(rhs_vectors, leaf_basis, outer_levels)
    outgoing, low, high, own_expand = lax.optimization_barrier((outgoing, low, high, leaf_expand))
    other_expand = lax.ppermute(own_expand, "rhs", swap)
    total_boxes = box_count * blocks
    first_box = lax.axis_index("blk") * box_count
    local = jnp.arange(box_count, dtype=jnp.int32)
    offsets = jnp.mod(near_list - (first_box + local)[:, None] + total_boxes // 2, total_boxes)
    index = (local[:, None] + 2 + offsets - total_boxes // 2).reshape(-1)
    arrived = lax.all_to_all(outgoing, ("blk", "rhs"), split_axis=0, concat_axis=0, tiled=True)
    near = near_field(index, near_blocks, boxes, low, high)
    arrived, near = lax.optimization_barrier((arrived, near))
    own, sent = inner(side, arrived, inner_levels)
    other = lax.ppermute(sent, "rhs", swap)
    result = expand_into(side, own, leaf_expand, near)
    return expand_into(1 - side, other, other_expand, result)


def solution(mesh):
    in_specs = (
        P("rhs", "blk"),
        P("blk", None, None),
        P(("blk", "rhs"), None, None),
        P(None, "blk", None),
        P(None, ("blk", "rhs"), None),
        P("blk", None, None, None),
        P("blk", None),
    )
    out_specs = P("rhs", "blk")
    return jax.shard_map(shards, mesh=mesh, in_specs=in_specs, out_specs=out_specs, check_vma=False)
```

```python
import jax
import jax.numpy as jnp
from jax import lax
from jax.experimental import pallas as pl
from jax.experimental.pallas import tpu as pltpu
from jax.sharding import PartitionSpec as P

RANK = 32
LEAF = 128
COLS = 32
F32 = jnp.float32
BF16 = jnp.bfloat16
NT = (((1,), (1,)), ((), ()))


NATURAL = (((0, 0), (1, 32), (2, 32), (3, 64)), ((4, 64), (5, 96), (6, 96), (7, 0)))
PAIRED = (((0, 0), (1, 32), (4, 0), (5, 32)), ((2, 96), (3, 0), (6, 96), (7, 0)))


def lane_block():
    return lax.broadcasted_iota(jnp.int32, (8, 128), 1) // RANK


def pick(choices):
    block = lane_block()
    low = jnp.where(block == 0, choices[0], choices[1])
    high = jnp.where(block == 2, choices[2], choices[3])
    return jnp.where(block < 2, low, high)


def factor_rows(factors, first):
    block = lax.broadcasted_iota(jnp.int32, (16, 128), 1) // RANK
    even = (block % 2) == 0
    left = block < 2
    rows = ([], [])
    for high in range(RANK // 4):
        kid0 = factors[pl.ds(first, 16), pl.ds(high * 128, 128)]
        kid1 = factors[pl.ds(first, 16), pl.ds(1024 + high * 128, 128)]
        outer = jnp.where(even, kid0, pltpu.roll(kid1, 32, 1))
        inner = jnp.where(even, pltpu.roll(kid0, 96, 1), kid1)
        outer_swap = pltpu.roll(outer, 64, 1)
        inner_swap = pltpu.roll(inner, 64, 1)
        for line in (
            jnp.where(left, outer, outer_swap),
            jnp.where(left, inner, inner_swap),
            jnp.where(left, outer_swap, outer),
            jnp.where(left, inner_swap, inner),
        ):
            wide = line.astype(F32)
            rows[0].append(wide[:8])
            rows[1].append(wide[8:])
    return [jnp.concatenate(part, axis=0).astype(BF16) for part in rows]


def split(value):
    high = value.astype(BF16)
    return high, (value - high.astype(F32)).astype(BF16)


def gathered(stage, layout):
    parts = []
    block = lane_block()
    shifts = sorted({shift for _, shift in layout})
    for part in range(4):
        total = None
        for shift in shifts:
            merged = None
            for lane, (freq, amount) in enumerate(layout):
                if amount != shift:
                    continue
                value = stage[pl.ds(part * 64 + freq, 8, stride=8), :]
                source = (lane - shift // 32) % 4
                merged = value if merged is None else jnp.where(block == source, value, merged)
            if shift:
                merged = pltpu.roll(merged, shift, 1)
            if total is None:
                total = merged
            else:
                mask = None
                for lane, (_, amount) in enumerate(layout):
                    if amount == shift:
                        here = block == lane
                        mask = here if mask is None else mask | here
                total = jnp.where(mask, merged, total)
        parts.append(total)
    return jnp.concatenate(parts, axis=0)


def put_state(state, at, value):
    high, low = split(value)
    state[0][at] = high
    state[1][at] = low


def run_level(step, layouts, factors, source, target, stage):
    sets = source[0].shape[0]
    blocks = source[0].shape[1] // 2
    for first in range(0, 8 * blocks, 16):
        both = factor_rows(factors, first)
        for part in range(2):
            m = first // 8 + part
            near = 2 * m - (m & (step - 1))
            far = near + step
            for which in range(sets):
                right = jnp.concatenate(
                    [
                        source[0][which, near],
                        source[0][which, far],
                        source[1][which, near],
                        source[1][which, far],
                    ],
                    axis=0,
                )
                slot = stage.at[m * sets + which]
                slot[...] = jnp.dot(both[part], right, preferred_element_type=F32)
                for half, layout in enumerate(layouts):
                    put_state(target, (which, 2 * m + half), gathered(slot, layout))


def level_step(level):
    return jnp.maximum(lax.shift_left(jnp.int32(1), jnp.maximum(level - 2, 0)), 1)


LEAF_STEPS = 4


def outer_kernel(
    rhs_hbm, basis_hbm, factors_hbm, boxes_out, out, rhs, basis, factors, stage, high0, low0, high1, low1, sems
):
    levels = factors.shape[0]
    count = basis.shape[0]
    per = count // LEAF_STEPS

    def leaf_copies(step):
        columns = pl.ds(pl.multiple_of(step * per * LEAF, LEAF), per * LEAF)
        boxes = pl.ds(step * per, per)
        return (
            pltpu.make_async_copy(rhs_hbm.at[:, columns], rhs.at[:, columns], sems.at[0, step]),
            pltpu.make_async_copy(basis_hbm.at[boxes], basis.at[boxes], sems.at[1, step]),
        )

    def level_copy(level):
        return pltpu.make_async_copy(factors_hbm.at[level], factors.at[level], sems.at[2, level])

    for step in range(LEAF_STEPS):
        for copy in leaf_copies(step):
            copy.start()
    for level in range(levels):
        level_copy(level).start()

    def leaf(step, carry):
        for copy in leaf_copies(step):
            copy.wait()
        for group in range(per // 8):
            first = step * per + group * 8
            at = pl.ds(pl.multiple_of(first * LEAF, LEAF), 8 * LEAF)
            columns = rhs[:, at].astype(BF16)
            pieces = [columns[:, box * LEAF : (box + 1) * LEAF] for box in range(8)]
            for box in range(8):
                boxes_out[first + box] = pieces[box]
            for kid in range(2):
                left = jnp.concatenate([basis[first + kid + 2 * i] for i in range(4)], axis=0)
                right = jnp.concatenate([pieces[kid + 2 * i] for i in range(4)], axis=0)
                value = lax.dot_general(left, right, NT, preferred_element_type=F32)
                parts = []
                for part in range(4):
                    at = [i * RANK + part * 8 for i in range(4)]
                    parts.append(pick([value[i : i + 8] for i in at]))
                at = step * (per // 4) + 2 * group + kid
                put_state((high0, low0), (0, at), jnp.concatenate(parts, axis=0))
        return carry

    lax.fori_loop(0, LEAF_STEPS, leaf, 0)

    even, odd = (high0, low0), (high1, low1)
    level_copy(0).wait()
    run_level(1, PAIRED, factors.at[0], even, odd, stage)

    def two_levels(pair, carry):
        level = 2 * pair + 1
        level_copy(level).wait()
        run_level(level_step(level), NATURAL, factors.at[level], odd, even, stage)
        level_copy(level + 1).wait()
        run_level(level_step(level + 1), NATURAL, factors.at[level + 1], even, odd, stage)
        return carry

    lax.fori_loop(0, (levels - 1) // 2, two_levels, 0)

    for block in range(count // 4):
        value = high1[0, block].astype(F32)
        for pair in range(2):
            parts = []
            for freq in (2 * pair, 2 * pair + 1):
                lines = []
                for part in range(4):
                    shift = (part - freq) * 32 % 128
                    line = value[part * 8 : part * 8 + 8]
                    lines.append(pltpu.roll(line, shift, 1) if shift else line)
                parts.append(pick(lines))
            at = pl.ds((2 * block + pair) * 16, 16)
            out[at, :] = jnp.concatenate(parts, axis=0).astype(BF16)


def outer(rhs, basis, factors):
    boxes = basis.shape[0]
    levels = factors.shape[0]
    state = pltpu.VMEM((1, boxes // 4, RANK, 128), BF16)
    whole = pl.BlockSpec(memory_space=pl.ANY)
    return pl.pallas_call(
        outer_kernel,
        in_specs=[whole, whole, whole],
        out_specs=[pl.BlockSpec(memory_space=pltpu.VMEM), pl.BlockSpec(memory_space=pltpu.VMEM)],
        out_shape=[
            jax.ShapeDtypeStruct((boxes, COLS, LEAF), BF16),
            jax.ShapeDtypeStruct((boxes * 8, 128), BF16),
        ],
        scratch_shapes=[
            pltpu.VMEM(rhs.shape, F32),
            pltpu.VMEM(basis.shape, BF16),
            pltpu.VMEM(factors.shape, BF16),
            pltpu.VMEM((boxes // 8, 256, 128), F32),
            state,
            state,
            state,
            state,
            pltpu.SemaphoreType.DMA((3, max(LEAF_STEPS, levels))),
        ],
        compiler_params=pltpu.CompilerParams(vmem_limit_bytes=56 * 2**20),
        cost_estimate=pl.CostEstimate(
            flops=4 * 10**8, bytes_accessed=8 * 10**6, transcendentals=0
        ),
        name="outer_levels",
    )(rhs, basis, factors)


NEAR_STEPS = 16


def near_kernel(index, blocks_hbm, boxes, low, high, out_hbm, wide, blocks, total, sems):
    count = boxes.shape[0]
    per = count // NEAR_STEPS

    def load(step):
        at = pl.ds(step * per, per)
        return pltpu.make_async_copy(blocks_hbm.at[at], blocks.at[at], sems.at[0, step])

    def store(step):
        at = pl.ds(pl.multiple_of(step * per * LEAF, LEAF), per * LEAF)
        return pltpu.make_async_copy(total.at[:, at], out_hbm.at[:, at], sems.at[1, step])

    for step in range(NEAR_STEPS):
        load(step).start()
    wide[pl.ds(2, count)] = boxes[...]
    for side in range(2):
        wide[side] = low[:, side * LEAF : (side + 1) * LEAF].astype(BF16)
        wide[count + 2 + side] = high[:, side * LEAF : (side + 1) * LEAF].astype(BF16)

    def body(step, carry):
        load(step).wait()
        zero = jnp.zeros((COLS, LEAF), BF16)
        for item in range(0, per, 2):
            pair = (step * per + item, step * per + item + 1)
            last = [wide[index[2, box]] for box in pair]
            left = jnp.concatenate(
                [
                    jnp.concatenate([last[0], zero], axis=1),
                    jnp.concatenate([zero, last[1]], axis=1),
                ],
                axis=0,
            )
            right = jnp.concatenate([blocks[box, 2] for box in pair], axis=1)
            third = lax.dot_general(left, right, NT, preferred_element_type=F32)
            for side, box in enumerate(pair):
                left = jnp.concatenate([wide[index[0, box]], wide[index[1, box]]], axis=1)
                right = jnp.concatenate([blocks[box, 0], blocks[box, 1]], axis=1)
                value = lax.dot_general(left, right, NT, preferred_element_type=F32)
                at = pl.ds(pl.multiple_of(box * LEAF, LEAF), LEAF)
                total[:, at] = value + third[side * COLS : (side + 1) * COLS]
        store(step).start()
        return carry

    lax.fori_loop(0, NEAR_STEPS, body, 0)
    for step in range(NEAR_STEPS):
        store(step).wait()


def near_field(index, blocks, boxes, low, high):
    count = blocks.shape[0]
    vmem = pl.BlockSpec(memory_space=pltpu.VMEM)
    anywhere = pl.BlockSpec(memory_space=pl.ANY)
    return pl.pallas_call(
        near_kernel,
        in_specs=[pl.BlockSpec(memory_space=pltpu.SMEM), anywhere, vmem, vmem, vmem],
        out_specs=anywhere,
        out_shape=jax.ShapeDtypeStruct((COLS, count * LEAF), F32),
        scratch_shapes=[
            pltpu.VMEM((count + 4, COLS, LEAF), BF16),
            pltpu.VMEM(blocks.shape, BF16),
            pltpu.VMEM((COLS, count * LEAF), F32),
            pltpu.SemaphoreType.DMA((2, NEAR_STEPS)),
        ],
        compiler_params=pltpu.CompilerParams(vmem_limit_bytes=56 * 2**20),
        cost_estimate=pl.CostEstimate(
            flops=5 * 10**8, bytes_accessed=16 * 10**6, transcendentals=0
        ),
        name="near_field",
    )(index, blocks, boxes, low, high)


def inner_kernel(side, arrived, factors_hbm, own, sent, factors, stage, high0, low0, high1, low1, sems):
    levels = factors.shape[0]
    sources = arrived.shape[0] // 16

    def level_copy(level):
        return pltpu.make_async_copy(factors_hbm.at[level], factors.at[level], sems.at[level])

    for level in range(levels):
        level_copy(level).start()

    low0[...] = jnp.zeros_like(low0)
    for first in range(0, sources, 8):
        both = [arrived[pl.ds((first + i) * 16, 16), :].astype(F32) for i in range(8)]
        for which in range(2):
            message = [value[which * 8 : which * 8 + 8] for value in both]
            for kid in range(2):
                parts = []
                for part in range(4):
                    lines = []
                    for i in range(4):
                        shift = (i - part) * 32 % 128
                        value = message[kid + 2 * i]
                        lines.append(pltpu.roll(value, shift, 1) if shift else value)
                    parts.append(pick(lines))
                high0[which, first // 4 + kid] = jnp.concatenate(parts, axis=0).astype(BF16)

    even, odd = (high0, low0), (high1, low1)
    level_copy(0).wait()
    run_level(1, PAIRED, factors.at[0], even, odd, stage)

    def two_levels(pair, carry):
        level = 2 * pair + 1
        level_copy(level).wait()
        run_level(level_step(level), NATURAL, factors.at[level], odd, even, stage)
        level_copy(level + 1).wait()
        run_level(level_step(level + 1), NATURAL, factors.at[level + 1], even, odd, stage)
        return carry

    lax.fori_loop(0, (levels - 2) // 2, two_levels, 0)
    level_copy(levels - 1).wait()
    last = factors.at[levels - 1]
    run_level(level_step(levels - 1), NATURAL, last, odd, even, stage)
    own[...] = high0[side[0]]
    sent[...] = high0[1 - side[0]]


def inner(side, arrived, factors):
    levels, sources, _ = factors.shape
    state = pltpu.VMEM((2, sources // 4, RANK, 128), BF16)
    return pl.pallas_call(
        inner_kernel,
        in_specs=[
            pl.BlockSpec(memory_space=pltpu.SMEM),
            pl.BlockSpec(memory_space=pltpu.VMEM),
            pl.BlockSpec(memory_space=pl.ANY),
        ],
        out_specs=[pl.BlockSpec(memory_space=pltpu.VMEM)] * 2,
        out_shape=[jax.ShapeDtypeStruct((sources // 4, RANK, 128), BF16)] * 2,
        scratch_shapes=[
            pltpu.VMEM(factors.shape, BF16),
            pltpu.VMEM((sources // 4, 256, 128), F32),
            state,
            state,
            state,
            state,
            pltpu.SemaphoreType.DMA((levels,)),
        ],
        compiler_params=pltpu.CompilerParams(vmem_limit_bytes=16 * 2**20),
        cost_estimate=pl.CostEstimate(
            flops=2 * 10**8, bytes_accessed=2 * 10**6, transcendentals=0
        ),
        name="inner_levels",
    )(side, arrived, factors)


EXPAND_STEPS = 4


def expand_kernel(side, coeffs, expand_hbm, near_hbm, out_hbm, expand, near, sems):
    boxes = expand.shape[0]
    per = boxes // EXPAND_STEPS
    width = per * LEAF

    def block(step):
        return pl.ds(pl.multiple_of(side[0] * (boxes * LEAF) + step * width, LEAF), width)

    def loads(step):
        at = pl.ds(step * per, per)
        here = pl.ds(step * width, width)
        return (
            pltpu.make_async_copy(expand_hbm.at[at], expand.at[at], sems.at[0, step]),
            pltpu.make_async_copy(near_hbm.at[:, block(step)], near.at[:, here], sems.at[1, step]),
        )

    def store(step):
        here = pl.ds(step * width, width)
        return pltpu.make_async_copy(near.at[:, here], out_hbm.at[:, block(step)], sems.at[2, step])

    for step in range(EXPAND_STEPS):
        for copy in loads(step):
            copy.start()
    turned = [coeffs[quad].astype(F32).T.astype(BF16) for quad in range(boxes // 4)]
    for step in range(EXPAND_STEPS):
        for copy in loads(step):
            copy.wait()
        for box in range(step * per, (step + 1) * per):
            part = box % 4
            at = pl.ds(box * LEAF, LEAF)
            near[:, at] += jnp.dot(
                turned[box // 4][part * COLS : (part + 1) * COLS],
                expand[box],
                preferred_element_type=F32,
            )
        store(step).start()
    for step in range(EXPAND_STEPS):
        store(step).wait()


def expand_into(side, coeffs, expand, near):
    boxes = expand.shape[0]
    anywhere = pl.BlockSpec(memory_space=pl.ANY)
    return pl.pallas_call(
        expand_kernel,
        in_specs=[
            pl.BlockSpec(memory_space=pltpu.SMEM),
            pl.BlockSpec(memory_space=pltpu.VMEM),
            anywhere,
            anywhere,
        ],
        out_specs=anywhere,
        out_shape=jax.ShapeDtypeStruct(near.shape, F32),
        scratch_shapes=[
            pltpu.VMEM(expand.shape, BF16),
            pltpu.VMEM((COLS, boxes * LEAF), F32),
            pltpu.SemaphoreType.DMA((3, EXPAND_STEPS)),
        ],
        input_output_aliases={3: 0},
        compiler_params=pltpu.CompilerParams(vmem_limit_bytes=8 * 2**20),
        cost_estimate=pl.CostEstimate(
            flops=2 * 10**7, bytes_accessed=3 * 10**6, transcendentals=0
        ),
        name="expand_boxes",
    )(side, coeffs, expand, near)


def shards(
    rhs_vectors, leaf_basis, leaf_expand, outer_levels, inner_levels, near_blocks, near_list
):
    box_count = leaf_basis.shape[0]
    blocks = lax.axis_size("blk")
    swap = [(0, 1), (1, 0)]
    side = lax.axis_index("rhs").astype(jnp.int32).reshape(1)

    width = 2 * LEAF
    forward = [(i, (i + 1) % blocks) for i in range(blocks)]
    backward = [(i, (i - 1) % blocks) for i in range(blocks)]
    low = lax.ppermute(rhs_vectors[:, -width:], "blk", forward)
    high = lax.ppermute(rhs_vectors[:, :width], "blk", backward)

    boxes, outgoing = outer(rhs_vectors, leaf_basis, outer_levels)
    outgoing, low, high, own_expand = lax.optimization_barrier((outgoing, low, high, leaf_expand))
    other_expand = lax.ppermute(own_expand, "rhs", swap)
    total_boxes = box_count * blocks
    first_box = lax.axis_index("blk") * box_count
    local = jnp.arange(box_count, dtype=jnp.int32)
    offsets = jnp.mod(near_list.T - (first_box + local) + total_boxes // 2, total_boxes)
    index = local + 2 + offsets - total_boxes // 2
    arrived = lax.all_to_all(outgoing, ("blk", "rhs"), split_axis=0, concat_axis=0, tiled=True)
    near = near_field(index, near_blocks, boxes, low, high)
    arrived, near = lax.optimization_barrier((arrived, near))
    own, sent = inner(side, arrived, inner_levels)
    other = lax.ppermute(sent, "rhs", swap)
    result = expand_into(side, own, leaf_expand, near)
    return expand_into(1 - side, other, other_expand, result)


def solution(mesh):
    in_specs = (
        P("rhs", "blk"),
        P("blk", None, None),
        P(("blk", "rhs"), None, None),
        P(None, "blk", None),
        P(None, ("blk", "rhs"), None),
        P("blk", None, None, None),
        P("blk", None),
    )
    out_specs = P("rhs", "blk")
    return jax.shard_map(shards, mesh=mesh, in_specs=in_specs, out_specs=out_specs, check_vma=False)
```
